128 devices in a mesh: node: 8 (over x, core), local: 16 (over y, z).
Axes of the slice: x: 4, y: 4, z: 4, core: 2. Of those that a mesh axis runs over, the one named last changes fastest.
Arguments:
- tokens: bfloat16 [2048, 7168], P('local'), may hold values from -6 to 6
- expert_ids: int32 [2048, 8], P('local'), may hold values from 0 to 31, all different within a row; in each aligned block of 128 rows (0 to 127, 128 to 255, ...) at most 48 rows name the same one
- expert_scores: float32 [2048, 8], P('local'), may hold values from 0.05 to 1
- w_gate: bfloat16 [32, 7168, 2048], P('local', None, 'node'), may hold values from -0.0625 to 0.0625
- w_up: bfloat16 [32, 7168, 2048], P('local', None, 'node'), may hold values from -0.0625 to 0.0625
- w_down: bfloat16 [32, 2048, 7168], P('local', None, 'node'), may hold values from -0.125 to 0.125
Outputs:
- moe_output: bfloat16 [2048, 7168], P('local', 'node')
The draws below stay inside these ranges and needn't reach their ends.
Inputs may be any that keep to these rules, and one draw needn't show every extreme that they name: `expert_ids`: each token names 8 different experts. Among the rows of one index of local no expert is named more than 48 times, and in every draw some index of local names some expert exactly 48 times.
All inputs are finite; a program needn't handle non-finite values.
Results may differ from the reference program's by a relative error of at most 0.012.
Values may be sent and summed in bfloat16 or wider, within the bound.
No kernel may reach another device: no remote copies, remote signals or barrier semaphores. Data moves between devices by JAX's collectives and lax.ppermute only.
A program may use at most 192 MiB of HBM per device.

```python
import math
import jax
import jax.numpy as jnp
import numpy as np
from jax import lax

D = 7168
FF = 2048
TOP = 8
TOK_DEV = 128
EXPERTS = 32
CAP = 48
TOKENS = 2048
N_LOCAL = 16


def level_of(key, shape, cuts, low, largest):
    def one(axis_at, blocks):
        steps = jax.random.uniform(jax.random.fold_in(jax.random.fold_in(key, 6), axis_at), (blocks,), jnp.float32, low / len(cuts), largest / len(cuts))
        return jnp.repeat(jnp.exp(steps), shape[axis_at] // blocks).reshape((-1,) + (1,) * (len(shape) - axis_at - 1))

    loudness = one(*cuts[0])
    for cut in cuts[1:]:
        loudness = loudness * one(*cut)
    return loudness


def deal_out(rng, own, number, rows, amount, top, limit, slope):
    sequence = jax.random.permutation(rng, amount)
    heavy_load, common = load_shares(amount, rows * top, limit, slope, True), load_shares(amount, rows * top, limit, slope, False)
    places = jnp.arange(amount)

    def named(sizes, turn):
        used = int((sizes > 0).sum())
        fixed = max(1, used // 4)
        passed = fixed + (places - fixed + turn * (used - fixed)) % max(1, amount - fixed)
        return jnp.zeros((amount,), jnp.int32).at[sequence[jnp.where(places < fixed, places, passed)]].set(jnp.asarray(sizes, jnp.int32))

    sizes = jnp.where(number % 4 == 0, named(heavy_load, number // 4), named(common, number - number // 4 - 1))
    mixed = jax.random.permutation(jax.random.fold_in(own, 3), amount)
    source_of, receiver = mixed[0:amount // 2 * 2:2], mixed[1:amount // 2 * 2:2]
    slack = jnp.minimum(sizes[source_of] - 1, limit - sizes[receiver]) // 2
    slack = jnp.where((source_of == sequence[0]) | (receiver == sequence[0]) | (sizes[receiver] == 0), 0, jnp.maximum(slack, 0))
    passed = jax.random.randint(jax.random.fold_in(own, 4), (amount // 2,), 0, 1 << 20) % (slack + 1)
    sizes = sizes.at[source_of].add(-passed).at[receiver].add(passed)
    labels = jnp.searchsorted(jnp.cumsum(sizes), jnp.arange(rows * top), side="right").astype(jnp.int32)
    listing = labels.reshape(top, rows).T
    listing = listing[jax.random.permutation(jax.random.fold_in(own, 1), rows)]
    turn = jax.random.randint(jax.random.fold_in(own, 2), (rows, 1), 0, top)
    return jnp.take_along_axis(listing, (jnp.arange(top)[None, :] + turn) % top, axis=1)


def load_shares(count, total, bound, skew, full):
    weights = [(1 << 20) // math.isqrt(standing ** skew) + 1 for standing in range(1, count + 1)]
    largest = bound if full else min(bound, max(-(-total // count), total * weights[0] // sum(weights)))
    least = 1 if total - largest >= count - 1 else 0
    holding, surplus = [largest] + [least] * (count - 1), total - largest - least * (count - 1)
    while surplus > 0:
        candidates = [i for i in range(1, count) if holding[i] < largest] or [i for i in range(1, count) if holding[i] < bound]
        mass, left = sum([weights[i] for i in candidates]), surplus
        for i in candidates:
            addition = min(bound - holding[i], max(1, left * weights[i] // mass), surplus)
            holding[i] = holding[i] + addition
            surplus = surplus - addition
    return np.array(holding)


def centred(key, shape, spread, most, cuts=(), kind=jnp.bfloat16):
    entries = spread * jax.random.normal(key, shape, jnp.float32)
    if cuts:
        entries = entries * level_of(key, shape, cuts, -0.22, 0.18)
    return jnp.clip(entries, -most, most).astype(kind)


def setup_inputs(seed: int = 0) -> dict:
    streams_of = jax.random.split(jax.random.key(seed), 7)
    tokens = centred(streams_of[0], (TOKENS, D), 1.0, 6.0, ((0, 16),))
    expert_ids_keys = jax.random.split(jax.random.fold_in(streams_of[1], 1), TOKENS // TOK_DEV)
    expert_ids_turns = jax.random.permutation(jax.random.fold_in(streams_of[1], 3), TOKENS // TOK_DEV)
    expert_ids = jax.vmap(lambda own, number: deal_out(jax.random.fold_in(streams_of[1], 2), own, number, TOK_DEV, EXPERTS, TOP, CAP, 2))(expert_ids_keys, expert_ids_turns).reshape((TOKENS, TOP))
    expert_scores = jnp.clip(jnp.exp(math.log(1.0) - 2.9957323 * jax.random.uniform(streams_of[2], (TOKENS, TOP), jnp.float32) ** level_of(streams_of[2], (TOKENS, TOP), ((0, 16),), -0.2, 0.2)), 0.05, 1.0)
    w_gate = centred(streams_of[3], (EXPERTS, D, FF), D ** -0.5, 0.0625, ((0, 16), (2, 8)))
    w_up = centred(streams_of[4], (EXPERTS, D, FF), D ** -0.5, 0.0625, ((0, 16), (2, 8)))
    w_down = centred(streams_of[5], (EXPERTS, FF, D), FF ** -0.5, 0.125, ((0, 16), (2, 8)))
    return {"tokens": tokens, "expert_ids": expert_ids, "expert_scores": expert_scores, "w_gate": w_gate, "w_up": w_up, "w_down": w_down}


def reference(tokens, expert_ids, expert_scores, w_gate, w_up, w_down):
    share = expert_scores / jnp.sum(expert_scores, axis=1, keepdims=True)
    flat_ids = expert_ids.reshape(-1)
    most_rows = N_LOCAL * CAP
    width = tokens.shape[1]
    tok_float = tokens.astype(jnp.float32)
    highest = lax.Precision.HIGHEST

    def one_expert(index):
        named = flat_ids == index
        found = jnp.nonzero(named, size=most_rows, fill_value=0)[0].astype(jnp.int32)
        count = jnp.sum(named.astype(jnp.int32))
        rows = tok_float[found // TOP]
        gate = jnp.dot(rows, w_gate[index].astype(jnp.float32), precision=highest)
        upper = jnp.dot(rows, w_up[index].astype(jnp.float32), precision=highest)
        hidden = lax.optimization_barrier((jax.nn.silu(gate) * upper).astype(jnp.bfloat16)).astype(jnp.float32)
        out = jnp.dot(hidden, w_down[index].astype(jnp.float32), precision=highest)
        out = lax.optimization_barrier(out.astype(jnp.bfloat16)).astype(jnp.float32)
        valid = jnp.arange(most_rows, dtype=jnp.int32) < count
        return jnp.where(valid[:, None], out, jnp.zeros_like(out)), found

    outputs, founds = lax.map(one_expert, jnp.arange(EXPERTS, dtype=jnp.int32))
    route_out = jnp.zeros((flat_ids.shape[0], width), jnp.float32)
    route_out = route_out.at[founds.reshape(-1)].add(outputs.reshape(-1, width))
    route_out = route_out.reshape(expert_ids.shape[0], TOP, width)
    mixed = jnp.sum(share[:, :, None] * route_out, axis=1)
    return mixed.astype(jnp.bfloat16)
```

```python
import functools

import jax
import jax.numpy as jnp
from jax import lax
from jax.experimental import pallas as pl
from jax.experimental.pallas import tpu as pltpu
from jax.sharding import PartitionSpec as P

BF = jnp.bfloat16
F32 = jnp.float32
AXES = ("node", "local")
SIDE = 4
CHUNKS = (
    tuple((dy, dz) for dy in (0, 1, 3) for dz in (0, 1, 3)),
    ((2, 0), (2, 1), (2, 3), (0, 2), (1, 2), (3, 2), (2, 2)),
)
CHUNKS = (tuple((dy, dz) for dy in range(4) for dz in range(4)),)


def device_at(x, c, y, z):
    return (x * 2 + c) * 16 + y * 4 + z


def hop(value, dx=0, dc=0, dy=0, dz=0):
    pairs = [
        (device_at(x, c, y, z), device_at((x + dx) % 4, (c + dc) % 2, (y + dy) % 4, (z + dz) % 4))
        for x in range(4)
        for c in range(2)
        for y in range(4)
        for z in range(4)
    ]
    return lax.ppermute(value, AXES, pairs)


def spread(own, first, second):
    own = own[None]
    near = {0: own, 1: hop(own, **{first: -1}), 3: hop(own, **{first: 1}), 2: hop(own, **{first: 2})}
    low = jnp.concatenate([near[0], near[1]])
    high = jnp.concatenate([near[2], near[3]])
    low_1 = hop(low, **{second: -1})
    high_3 = hop(high, **{second: 1})
    high_1 = hop(high, **{second: -1})
    low_3 = hop(low, **{second: 1})
    low_2 = hop(low_1, **{second: -1})
    high_2 = hop(high_3, **{second: 1})
    found = {(d, 0): (near[d], 0) for d in range(4)}
    for e, lower, upper in ((1, low_1, high_1), (3, low_3, high_3), (2, low_2, high_2)):
        found[0, e], found[1, e] = (lower, 0), (lower, 1)
        found[2, e], found[3, e] = (upper, 0), (upper, 1)
    return found


def expand_kernel(count, cap, started, *refs):
    blocks, (table, weight), rest = refs[:count], refs[count : count + 2], refs[count + 2 :]
    if started:
        before, out, rows = rest
    else:
        before, (out, rows) = None, rest
    for s in range(count):
        picked = jnp.dot(table[s], blocks[s][0], preferred_element_type=F32).astype(BF)
        for e in range(2):
            rows[e, s * cap : (s + 1) * cap, :] = picked[e * cap : (e + 1) * cap]
    first = pl.program_id(0) == 0
    for e in range(2):
        part = jnp.dot(rows[e], weight[e], preferred_element_type=F32)

        @pl.when(first)
        def _():
            out[e] = part + before[e] if started else part

        @pl.when(jnp.logical_not(first))
        def _():
            out[e] += part


def expand(sources, table, weight, before=None):
    count = len(sources)
    cap = table.shape[1] // 2
    depth, width = weight.shape[1:]
    step = 896
    rows = count * cap

    def at(index):
        return pl.BlockSpec((1, 128, step), lambda k: (index, 0, k))

    whole = pl.BlockSpec((2, rows, width), lambda k: (0, 0, 0))
    specs = [at(i) for _, i in sources] + [
        pl.BlockSpec(table.shape, lambda k: (0, 0, 0)),
        pl.BlockSpec((2, step, width), lambda k: (0, k, 0)),
    ]
    given = [a for a, _ in sources] + [table, weight]
    if before is not None:
        specs.append(whole)
        given.append(before)
    return pl.pallas_call(
        functools.partial(expand_kernel, count, cap, before is not None),
        grid=(depth // step,),
        in_specs=specs,
        out_specs=whole,
        out_shape=jax.ShapeDtypeStruct((2, rows, width), F32),
        scratch_shapes=[pltpu.VMEM((2, rows, step), BF)],
        compiler_params=pltpu.CompilerParams(vmem_limit_bytes=56 * 2**20),
        cost_estimate=pl.CostEstimate(
            flops=4 * rows * depth * width + 4 * rows * 128 * depth,
            bytes_accessed=count * 128 * depth * 2 + 4 * depth * width + 8 * rows * width,
            transcendentals=0,
        ),
    )(*given)


def contract_kernel(count, cap, pieces, *refs):
    hidden, (weight, table, out) = refs[:pieces], refs[pieces:]
    depth = hidden[0].shape[-1]
    results = []
    for e in range(2):
        total = None
        for p in range(pieces):
            part = jnp.dot(
                hidden[p][e], weight[e, p * depth : (p + 1) * depth, :], preferred_element_type=F32
            )
            total = part if total is None else total + part
        results.append(total.astype(BF))
    for s in range(count):
        rows = jnp.concatenate([r[s * cap : (s + 1) * cap] for r in results])
        out[s] = jnp.dot(table[s], rows, preferred_element_type=F32).astype(BF)


def contract(hidden, weight, table):
    count, tokens, double = table.shape
    cap = double // 2
    pieces = len(hidden)
    rows = count * cap
    width = weight.shape[2]
    return pl.pallas_call(
        functools.partial(contract_kernel, count, cap, pieces),
        in_specs=[pl.BlockSpec(memory_space=pltpu.VMEM)] * (pieces + 2),
        out_specs=pl.BlockSpec(memory_space=pltpu.VMEM),
        out_shape=jax.ShapeDtypeStruct((count, tokens, width), BF),
        compiler_params=pltpu.CompilerParams(vmem_limit_bytes=56 * 2**20),
        cost_estimate=pl.CostEstimate(
            flops=4 * rows * weight.shape[1] * width + 4 * rows * tokens * width,
            bytes_accessed=4 * rows * weight.shape[1]
            + 4 * weight.shape[1] * width
            + count * tokens * width * 2,
            transcendentals=0,
        ),
    )(*hidden, weight, table)


def body(tokens, expert_ids, expert_scores, w_gate, w_up, w_down):
    tok_rows, top_count = expert_ids.shape
    width = tokens.shape[1]
    half = width // 2
    exp_local = w_gate.shape[0]
    cap = 48
    node, place = lax.axis_index("node"), lax.axis_index("local")
    x, c = node // 2, node % 2
    y, z = place // SIDE, place % SIDE

    mine = lax.dynamic_slice_in_dim(tokens, c * half, half, axis=1)
    found_a = spread(mine[:, : half // 2], "dy", "dz")
    found_b = spread(mine[:, half // 2 :], "dz", "dy")

    both = jnp.concatenate([w_gate, w_up], axis=2)
    own_w = lax.dynamic_slice_in_dim(both, c * half, half, axis=1)
    other_w = hop(lax.dynamic_slice_in_dim(both, (1 - c) * half, half, axis=1), dc=1)
    weight = jnp.concatenate([own_w, other_w], axis=2)

    units = w_gate.shape[2]
    order = [(0, 0), (3, 0), (1, 0), (2, 0), (0, 1), (3, 1), (1, 1), (2, 1)]
    down = jnp.concatenate(
        [
            lax.dynamic_slice_in_dim(
                w_down, (((x + dx) % 4) * 2 + (c + dc) % 2) * units, units, axis=1
            )
            for dx, dc in order
        ],
        axis=1,
    )

    share = expert_scores / jnp.sum(expert_scores, axis=1, keepdims=True)
    named = lax.all_gather(
        jnp.concatenate([expert_ids.astype(F32), share], axis=1), "local", axis=0
    )
    offsets = [o for chunk in CHUNKS for o in chunk]
    rel = jnp.stack([((y + dy) % 4) * 4 + (z + dz) % 4 for dy, dz in offsets])
    named = named[rel]
    ids, shares = named[..., :top_count], named[..., top_count:]
    wanted = (place * exp_local + jnp.arange(exp_local)).astype(F32)
    hit = ids[:, None] == wanted[None, :, None, None]
    picked = jnp.any(hit, axis=-1)
    weigh = jnp.sum(jnp.where(hit, shares[:, None], 0.0), axis=-1)
    earlier = jnp.tril(jnp.ones((tok_rows, tok_rows), BF), -1)
    rank = jnp.einsum("set,ut->seu", picked.astype(BF), earlier, preferred_element_type=F32)
    chosen = jnp.where(picked, rank, -1.0)
    slot = chosen[:, :, None, :] == jnp.arange(cap, dtype=F32)[None, None, :, None]
    row_share = jnp.sum(jnp.where(slot, weigh[:, :, None, :], 0.0), axis=-1)
    gather_table = slot.astype(BF).reshape(16, exp_local * cap, tok_rows)
    combine_table = (
        (chosen[:, :, :, None] == jnp.arange(cap, dtype=F32)).astype(BF).transpose(0, 2, 1, 3)
    ).reshape(16, tok_rows, exp_local * cap)

    parts = {}
    at = 0
    for chunk in CHUNKS:
        count = len(chunk)
        here = slice(at, at + count)
        at += count
        table = gather_table[here]
        depth = half // 2
        total = expand([found_a[dy, dz] for dy, dz in chunk], table, weight[:, :depth])
        total = expand([found_b[dz, dy] for dy, dz in chunk], table, weight[:, depth:], total)
        arrived = hop(total[:, :, 2 * units :].astype(BF), dc=1).astype(F32)
        total = total[:, :, : 2 * units] + arrived
        gate, upper = total[..., :units], total[..., units:]
        scale = row_share[here].transpose(1, 0, 2).reshape(exp_local, count * cap, 1)
        hidden = (jax.nn.silu(gate) * upper * scale).astype(BF)
        plane = [hidden, hop(hidden, dx=1), hop(hidden, dx=-1), hop(hidden, dx=2)]
        pieces = plane + [hop(p, dc=1) for p in plane]
        out = contract(pieces, down, combine_table[here])
        for s, offset in enumerate(chunk):
            parts[offset] = (out, s)

    rows_half = tok_rows // 2

    def back(first, second, rows):
        def part(d, e):
            offset = (d, e) if first == "dy" else (e, d)
            out, s = parts[offset]
            return out[s, rows]

        sums = [part(0, e).astype(F32) for e in range(4)]
        for d in (1, 3, 2):
            bundle = hop(jnp.stack([part(d, e) for e in range(4)]), **{first: d})
            sums = [a + bundle[e].astype(F32) for e, a in enumerate(sums)]
        final = sums[0]
        for e in (1, 3, 2):
            final = final + hop(sums[e].astype(BF), **{second: e}).astype(F32)
        return final.astype(BF)

    return jnp.concatenate(
        [back("dz", "dy", slice(0, rows_half)), back("dy", "dz", slice(rows_half, tok_rows))]
    )


def solution(mesh):
    placed = (
        P("local", None),
        P("local", None),
        P("local", None),
        P("local", None, "node"),
        P("local", None, "node"),
        P("local", None, "node"),
    )
    return jax.shard_map(
        body, mesh=mesh, in_specs=placed, out_specs=P("local", "node"), check_vma=False
    )
```

```python
import functools

import jax
import jax.numpy as jnp
from jax import lax
from jax.experimental import pallas as pl
from jax.experimental.pallas import tpu as pltpu
from jax.sharding import PartitionSpec as P

BF = jnp.bfloat16
F32 = jnp.float32
AXES = ("node", "local")
SIDE = 4
CAP = 48
META = 128
STEP = 896
VMEM_LIMIT = 56 * 2**20
CHUNKS = (
    ((0, 0), (1, 1), (3, 3), (0, 3), (3, 0)),
    ((2, 2), (2, 0), (0, 2), (2, 1), (1, 2)),
    ((3, 1), (2, 3), (1, 3), (3, 2), (0, 1), (1, 0)),
)


def device_at(x, c, y, z):
    return (x * 2 + c) * 16 + y * 4 + z


def hop(value, dx=0, dc=0, dy=0, dz=0):
    pairs = [
        (device_at(x, c, y, z), device_at((x + dx) % 4, (c + dc) % 2, (y + dy) % 4, (z + dz) % 4))
        for x in range(4)
        for c in range(2)
        for y in range(4)
        for z in range(4)
    ]
    return lax.ppermute(value, AXES, pairs)


def spread_first(own, first):
    own = own[None]
    return {
        0: own,
        1: hop(own, **{first: -1}),
        3: hop(own, **{first: 1}),
        2: hop(own, **{first: 2}),
    }


def spread_second(near, second):
    pair = {"l": jnp.concatenate([near[1], near[2]]), "r": jnp.concatenate([near[3], near[0]])}
    l_1 = hop(pair["l"], **{second: -1})
    r_3 = hop(pair["r"], **{second: 1})
    l_2 = hop(l_1, **{second: -1})
    r_2 = hop(r_3, **{second: 1})
    r_1 = hop(pair["r"], **{second: -1})
    l_3 = hop(pair["l"], **{second: 1})
    found = {(d, 0): (near[d], 0) for d in range(4)}
    for e, left, right in ((1, l_1, r_1), (3, l_3, r_3), (2, l_2, r_2)):
        found[1, e], found[2, e] = (left, 0), (left, 1)
        found[3, e], found[0, e] = (right, 0), (right, 1)
    return found


def expand_kernel(count, halves, _, *refs):
    blocks_a, blocks_b = refs[:count], refs[count : 2 * count]
    table, *weights = refs[2 * count : 2 * count + 5]
    own, other, rows, total = refs[2 * count + 5 :]
    k = pl.program_id(0)

    def pick(blocks):
        for s in range(count):
            picked = jnp.dot(table[s], blocks[s][0], preferred_element_type=F32).astype(BF)
            for e in range(2):
                rows[e, s * CAP : (s + 1) * CAP, :] = picked[e * CAP : (e + 1) * CAP]

    @pl.when(k < halves)
    def _():
        pick(blocks_a)

    @pl.when(k >= halves)
    def _():
        pick(blocks_b)

    @pl.when(k == 0)
    def _():
        total[...] = jnp.zeros_like(total)

    for e in range(2):
        for n, weight in enumerate(weights):
            at = slice(n * weight.shape[2], (n + 1) * weight.shape[2])
            total[e, :, at] += jnp.dot(rows[e], weight[e], preferred_element_type=F32)

    @pl.when(k == 2 * halves - 1)
    def _():
        split = own.shape[2]
        own[...] = total[:, :, :split]
        other[...] = total[:, :, split:].astype(BF)


def expand(core, sources_a, sources_b, table, own_weights, other_weights):
    count = len(sources_a)
    units = own_weights[0].shape[2]
    rows = count * CAP
    half = other_weights[0].shape[1]
    halves = half // 2 // STEP

    def part_a(index):
        return pl.BlockSpec((1, 128, STEP), lambda k, c: (index, 0, jnp.minimum(k, halves - 1)))

    def part_b(index):
        return pl.BlockSpec((1, 128, STEP), lambda k, c: (index, 0, jnp.maximum(k - halves, 0)))

    result = pl.BlockSpec((2, rows, 2 * units), lambda k, c: (0, 0, 0))
    own_spec = pl.BlockSpec((2, STEP, units), lambda k, c: (0, c[0] * 2 * halves + k, 0))
    other_spec = pl.BlockSpec((2, STEP, units), lambda k, c: (0, k, 0))
    return pl.pallas_call(
        functools.partial(expand_kernel, count, halves),
        grid_spec=pltpu.PrefetchScalarGridSpec(
            num_scalar_prefetch=1,
            grid=(2 * halves,),
            in_specs=[part_a(i) for _, i in sources_a]
            + [part_b(i) for _, i in sources_b]
            + [pl.BlockSpec(table.shape, lambda k, c: (0, 0, 0))]
            + [own_spec] * 2
            + [other_spec] * 2,
            out_specs=[result, result],
            scratch_shapes=[
                pltpu.VMEM((2, rows, STEP), BF),
                pltpu.VMEM((2, rows, 4 * units), F32),
            ],
        ),
        out_shape=[
            jax.ShapeDtypeStruct((2, rows, 2 * units), F32),
            jax.ShapeDtypeStruct((2, rows, 2 * units), BF),
        ],
        compiler_params=pltpu.CompilerParams(vmem_limit_bytes=VMEM_LIMIT),
        cost_estimate=pl.CostEstimate(
            flops=16 * rows * half * units + 4 * rows * 128 * half,
            bytes_accessed=count * 256 * half + 16 * half * units + 24 * rows * units,
            transcendentals=0,
        ),
    )(
        core,
        *[a for a, _ in sources_a],
        *[a for a, _ in sources_b],
        table,
        *own_weights,
        *other_weights,
    )


def contract_kernel(count, pieces, stacked, blocks, *refs):
    hidden, (weight, table), outs = refs[:stacked], refs[stacked : stacked + 2], refs[stacked + 2 :]
    depth = hidden[0].shape[-1]
    results = []
    for e in range(2):
        total = None
        for p in range(pieces):
            value = hidden[0][p, e] if stacked == 1 else hidden[p][e]
            start = pl.multiple_of(blocks[p] * depth, depth)
            part = jnp.dot(value, weight[e, pl.ds(start, depth), :], preferred_element_type=F32)
            total = part if total is None else total + part
        results.append(total.astype(BF))
    for s in range(count):
        rows = jnp.concatenate([r[s * CAP : (s + 1) * CAP] for r in results])
        outs[s][...] = jnp.dot(table[s], rows, preferred_element_type=F32).astype(BF)


def contract(blocks, hidden, weight, table):
    count, tokens, _ = table.shape
    pieces = blocks.shape[0]
    rows = count * CAP
    width = weight.shape[2]
    in_vmem = pl.BlockSpec(memory_space=pltpu.VMEM)
    return pl.pallas_call(
        functools.partial(contract_kernel, count, pieces, len(hidden)),
        in_specs=[pl.BlockSpec(memory_space=pltpu.SMEM)] + [in_vmem] * (len(hidden) + 2),
        out_specs=[in_vmem] * count,
        out_shape=[jax.ShapeDtypeStruct((tokens, width), BF)] * count,
        compiler_params=pltpu.CompilerParams(vmem_limit_bytes=VMEM_LIMIT),
        cost_estimate=pl.CostEstimate(
            flops=4 * rows * weight.shape[1] * width + 4 * rows * tokens * width,
            bytes_accessed=4 * rows * weight.shape[1]
            + 4 * weight.shape[1] * width
            + count * tokens * width * 2,
            transcendentals=0,
        ),
    )(blocks, *hidden, weight, table)


def tables(meta, place):
    top = 8
    ids = meta[..., :top]
    shares = meta[..., top : 2 * top] + meta[..., 2 * top : 3 * top]
    count, tokens, _ = ids.shape
    wanted = (place * 2 + jnp.arange(2)).astype(F32)
    hit = ids[:, None] == wanted[None, :, None, None]
    picked = jnp.any(hit, axis=-1)
    weigh = jnp.sum(jnp.where(hit, shares[:, None], 0.0), axis=-1)
    earlier = jnp.tril(jnp.ones((tokens, tokens), BF), -1)
    rank = jnp.einsum("set,ut->seu", picked.astype(BF), earlier, preferred_element_type=F32)
    chosen = jnp.where(picked, rank, -1.0)
    slot = chosen[:, :, None, :] == jnp.arange(CAP, dtype=F32)[None, None, :, None]
    row_share = jnp.sum(jnp.where(slot, weigh[:, :, None, :], 0.0), axis=-1)
    gather_table = slot.astype(BF).reshape(count, 2 * CAP, tokens)
    combine_table = (
        (chosen[:, :, :, None] == jnp.arange(CAP, dtype=F32)).astype(BF).transpose(0, 2, 1, 3)
    ).reshape(count, tokens, 2 * CAP)
    scale = row_share.transpose(1, 0, 2).reshape(2, count * CAP, 1)
    return gather_table, combine_table, scale


def body(tokens, expert_ids, expert_scores, w_gate, w_up, w_down):
    width = tokens.shape[1]
    half = width // 2
    part = half // 2
    units = w_gate.shape[2]
    node, place = lax.axis_index("node"), lax.axis_index("local")
    x, c = node // 2, node % 2
    core = c.astype(jnp.int32).reshape(1)

    share = expert_scores / jnp.sum(expert_scores, axis=1, keepdims=True)
    high = share.astype(BF)
    low = (share - high.astype(F32)).astype(BF)
    meta = jnp.concatenate([expert_ids.astype(BF), high, low], axis=1)
    meta = jnp.pad(meta, ((0, 0), (0, META - meta.shape[1])))

    mine_a = lax.dynamic_slice_in_dim(tokens, c * half, part, axis=1)
    mine_b = lax.dynamic_slice_in_dim(tokens, c * half + part, part, axis=1)
    near_a = spread_first(jnp.concatenate([mine_a, meta], axis=1), "dy")
    near_b = spread_first(mine_b, "dz")

    gate_w, up_w, near_a[1], near_b[1] = lax.optimization_barrier(
        (w_gate, w_up, near_a[1], near_b[1])
    )
    other_gate = hop(lax.dynamic_slice_in_dim(gate_w, (1 - c) * half, half, axis=1), dc=1)
    other_up = hop(lax.dynamic_slice_in_dim(up_w, (1 - c) * half, half, axis=1), dc=1)

    found_a = spread_second(near_a, "dz")
    found_b = spread_second(near_b, "dy")

    blocks_abs = jnp.arange(8, dtype=jnp.int32)
    blocks_rel = jnp.stack(
        [
            ((x + dx) % 4) * 2 + (c + dc) % 2
            for dx, dc in ((0, 0), (3, 0), (1, 0), (2, 0), (0, 1), (3, 1), (1, 1), (2, 1))
        ]
    ).astype(jnp.int32)

    final = None
    for number, chunk in enumerate(CHUNKS):
        sources_a = [found_a[dy, dz] for dy, dz in chunk]
        sources_b = [found_b[dz, dy] for dy, dz in chunk]
        metas = jnp.stack([a[i, :, part : part + 24] for a, i in sources_a]).astype(F32)
        gather_table, combine_table, scale = tables(metas, place)
        total, away = expand(
            core, sources_a, sources_b, gather_table, (w_gate, w_up), (other_gate, other_up)
        )
        total = total + hop(away, dc=1).astype(F32)
        gate, upper = total[..., :units], total[..., units:]
        hidden = (jax.nn.silu(gate) * upper * scale).astype(BF)
        if number < len(CHUNKS) - 1:
            pieces = [lax.all_gather(hidden, "node", axis=0)]
            outs = contract(blocks_abs, pieces, w_down, combine_table)
        else:
            plane = [hidden, hop(hidden, dx=1), hop(hidden, dx=-1), hop(hidden, dx=2)]
            pieces = plane + [hop(p, dc=1) for p in plane]
            outs = contract(blocks_rel, pieces, w_down, combine_table)
        for (dy, dz), out in zip(chunk, outs):
            arrived = out if (dy, dz) == (0, 0) else hop(out, dy=dy, dz=dz)
            arrived = arrived.astype(F32)
            final = arrived if final is None else final + arrived
    return final.astype(BF)


def solution(mesh):
    placed = (
        P("local", None),
        P("local", None),
        P("local", None),
        P("local", None, "node"),
        P("local", None, "node"),
        P("local", None, "node"),
    )
    return jax.shard_map(
        body, mesh=mesh, in_specs=placed, out_specs=P("local", "node"), check_vma=False
    )
```
